32 devices in a mesh: grp: 2 (over x), wide: 8 (over z, y), narrow: 2 (over core).
Axes of the slice: x: 2, y: 2, z: 4, core: 2. Of those that a mesh axis runs over, the one named last changes fastest.
Arguments:
- tokens: bfloat16 [2, 64, 8192], P(None, ('grp', 'wide'), 'narrow'), parts along dimension 1, may hold values from -6 to 6
- gate_weight: bfloat16 [8192, 26624], P('narrow', 'wide'), may hold values from -0.0625 to 0.0625
- up_weight: bfloat16 [8192, 26624], P('narrow', 'wide'), may hold values from -0.0625 to 0.0625
- down_weight: bfloat16 [26624, 8192], P('wide', 'narrow'), may hold values from -0.0390625 to 0.0390625
Outputs:
- mixed: bfloat16 [2, 64, 8192], P(None, ('grp', 'wide'), 'narrow'), parts along dimension 1
The draws below stay inside these ranges and needn't reach their ends.
There are 2 independent parts, one for each index of `grp`. The reference program is written for one: setup_inputs(seed, part) draws one part's arguments, and reference() takes and returns one part's arrays. A program takes and returns all parts, laid end to end along the dimension named above; an argument that names none is the same for every part. Nothing has to cross between parts.
All inputs are finite; a program needn't handle non-finite values.
Results may differ from the reference program's by a relative error of at most 0.0075.
Values may be sent and summed in bfloat16 or wider, within the bound.
A program may use at most 256 MiB of HBM per device.

```python
import jax
import jax.numpy as jnp

D = 8192
FF = 26624
STEPS = 2
ROWS = 32


def shard_levels(rng, shape, pieces, low, top_value):
    gain = 1.0
    for dim, shards_of in pieces:
        draws = jax.random.uniform(jax.random.fold_in(jax.random.fold_in(rng, 6), dim), (shards_of,), jnp.float32, low / len(pieces), top_value / len(pieces))
        gain = gain * jnp.repeat(jnp.exp(draws), shape[dim] // shards_of).reshape((-1,) + (1,) * (len(shape) - 1 - dim))
    return gain


def scatter_about(key, shape, deviation, bound, pieces=(), kind=jnp.bfloat16):
    result = jax.random.normal(key, shape, jnp.float32) * deviation
    if len(pieces) > 0:
        result = shard_levels(key, shape, pieces, -0.22, 0.18) * result
    return jnp.clip(result, min=-bound, max=bound).astype(kind)


def setup_inputs(seed: int = 0, part: int = 0) -> dict:
    arg_keys = jax.random.split(jax.random.key(seed), 5)
    part_keys = jax.random.split(jax.random.fold_in(arg_keys[4], part), 5)
    return {
        "tokens": scatter_about(part_keys[0], (STEPS, ROWS, D), 1.0, 6.0, ((1, 8), (2, 2))),
        "gate_weight": scatter_about(arg_keys[1], (D, FF), D ** -0.5, 0.0625, ((0, 2), (1, 8))),
        "up_weight": scatter_about(arg_keys[2], (D, FF), D ** -0.5, 0.0625, ((0, 2), (1, 8))),
        "down_weight": scatter_about(arg_keys[3], (FF, D), FF ** -0.5, 0.0390625, ((0, 8), (1, 2))),
    }


def reference(tokens, gate_weight, up_weight, down_weight):
    outputs = []
    previous = None
    for step_index in range(STEPS):
        if previous is None:
            rows_now = tokens[step_index]
        else:
            rows_now = (tokens[step_index].astype(jnp.float32) + previous.astype(jnp.float32)).astype(jnp.bfloat16)
        gate = jnp.dot(rows_now, gate_weight, preferred_element_type=jnp.float32)
        up_part = jnp.dot(rows_now, up_weight, preferred_element_type=jnp.float32)
        hidden = (jax.nn.silu(gate) * up_part).astype(jnp.bfloat16)
        previous = jnp.dot(hidden, down_weight, preferred_element_type=jnp.float32).astype(jnp.bfloat16)
        outputs.append(previous)
    return jnp.stack(outputs)
```

```python
import functools

import jax
import jax.numpy as jnp
from jax import lax
from jax.experimental import pallas as pl
from jax.experimental.pallas import tpu as pltpu
from jax.sharding import PartitionSpec as P

F32 = jnp.float32
BF16 = jnp.bfloat16
MESH = pl.DeviceIdType.MESH
STRIP = 256
RING = 3


def kernel(
    n, groups, halves, unit_tile, tok_ref, gate_ref, up_ref, down_ref, out_ref,
    pool, tok_all, rows_in, rows_next, own_sums, send_sums, recv_sums, hidden,
    part_send, part_recv, piece, mixed_all, tail_send,
    load_sem, tok_own_sem, tok_send_sem, tok_recv_sem, pair_send_sem, pair_recv_sem,
    part_send_sem, part_recv_sem, gather_send_sem, gather_recv_sem, tail_send_sem, tail_recv_sem,
):
    steps, per_dev, width = tok_ref.shape
    units = gate_ref.shape[1]
    chunks = units // unit_tile
    strips = width // STRIP
    row_blocks = n // groups
    block_rows = per_dev * groups
    rows = n * per_dev
    me = lax.axis_index("wide")
    core = lax.axis_index("narrow")
    peer = {"narrow": 1 - core}
    my_row_block, my_group = me // groups, me % groups

    def gate_load(j):
        cols = pl.ds(pl.multiple_of(j * unit_tile, unit_tile), unit_tile)
        return [
            pltpu.make_async_copy(
                w.at[:, cols], pool.at[2 * j + i, pl.ds(0, width), pl.ds(0, unit_tile)],
                load_sem.at[2 * j + i],
            )
            for i, w in enumerate((gate_ref, up_ref))
        ]

    def strip_block(j):
        return (me + 1 + j // halves) % groups

    def down_load(j, slot):
        first = strip_block(j) * halves + j % halves
        cols = pl.ds(pl.multiple_of(first * STRIP, STRIP), STRIP)
        return pltpu.make_async_copy(
            down_ref.at[:, cols], pool.at[slot, pl.ds(0, units), pl.ds(0, STRIP)], load_sem.at[slot]
        )

    def start_gate(j, carry):
        for copy in gate_load(j):
            copy.start()
        return carry

    lax.fori_loop(0, chunks, start_gate, 0)
    for j in range(RING):
        down_load(j, 2 * chunks + j).start()

    barrier = pltpu.get_barrier_semaphore()

    def greet(i, carry):
        pl.semaphore_signal(barrier, inc=1, device_id={"wide": (me + i) % n}, device_id_type=MESH)
        return carry

    lax.fori_loop(1, n, greet, 0)
    pl.semaphore_signal(barrier, inc=1, device_id=peer, device_id_type=MESH)
    pl.semaphore_wait(barrier, n)

    def tok_copy(s, to, slot):
        return pltpu.make_async_remote_copy(
            src_ref=tok_ref.at[s], dst_ref=tok_all.at[s, slot],
            send_sem=tok_send_sem.at[s, to], recv_sem=tok_recv_sem.at[s, slot],
            device_id={"wide": to}, device_id_type=MESH,
        )

    for s in range(steps):
        own = pltpu.make_async_copy(tok_ref.at[s], tok_all.at[s, me], tok_own_sem.at[s])
        own.start()

        def send_tok(i, carry, s=s):
            tok_copy(s, (me + i) % n, me).start()
            return carry

        lax.fori_loop(1, n, send_tok, 0)

    def place_tokens(s, target):
        pltpu.make_async_copy(tok_ref.at[s], tok_all.at[s, me], tok_own_sem.at[s]).wait()

        def arrive(i, carry):
            source = (me + i) % n
            tok_copy(s, source, source).wait_recv()
            return carry

        lax.fori_loop(1, n, arrive, 0)
        per = 16 // per_dev

        def place(i, carry):
            value = jnp.concatenate(
                [tok_all[s, i * per + t].astype(F32) for t in range(per)], axis=0
            ).astype(BF16)
            at = pl.ds(pl.multiple_of(i * 16, 16), 16)
            for b in range(strips):
                target[b, at, :] = value[:, b * STRIP:(b + 1) * STRIP]
            return carry

        lax.fori_loop(0, rows // 16, place, 0)

    def pair_copy(s, j):
        return pltpu.make_async_remote_copy(
            src_ref=send_sums.at[s, j], dst_ref=recv_sums.at[s, j],
            send_sem=pair_send_sem.at[s, j], recv_sem=pair_recv_sem.at[s, j],
            device_id=peer, device_id_type=MESH,
        )

    def part_copy(s, j, r, owner, slot):
        return pltpu.make_async_remote_copy(
            src_ref=part_send.at[s, j, r],
            dst_ref=part_recv.at[s, slot, j % halves],
            send_sem=part_send_sem.at[s, j, r], recv_sem=part_recv_sem.at[s, slot, j % halves],
            device_id={"wide": owner}, device_id_type=MESH,
        )

    def gather_copy(h, to, slot):
        return pltpu.make_async_remote_copy(
            src_ref=piece.at[h], dst_ref=mixed_all.at[slot, h],
            send_sem=gather_send_sem.at[to, h], recv_sem=gather_recv_sem.at[slot, h],
            device_id={"wide": to}, device_id_type=MESH,
        )

    def tail_copy(h, t, group):
        cols = pl.ds(pl.multiple_of((group * halves + h) * STRIP, STRIP), STRIP)
        return pltpu.make_async_remote_copy(
            src_ref=tail_send.at[t, h], dst_ref=out_ref.at[1, :, cols],
            send_sem=tail_send_sem.at[t, h], recv_sem=tail_recv_sem.at[group, h],
            device_id={"wide": my_row_block * groups + t}, device_id_type=MESH,
        )

    def gate_up(s):
        def body(j, carry):
            if s == 0:
                for copy in gate_load(j):
                    copy.wait()
            x = jnp.concatenate([rows_in[b] for b in range(strips)], axis=1)
            sums = [
                jnp.dot(x, pool[2 * j + i, pl.ds(0, width), pl.ds(0, unit_tile)], preferred_element_type=F32)
                for i in range(2)
            ]
            for i in range(2):
                own_sums[j, i] = sums[i]
                send_sums[s, j, i] = sums[i].astype(BF16)
            pair_copy(s, j).start()
            if s == 1:
                for i in range(2):
                    @pl.when(2 * j + i < strips - RING)
                    def _():
                        down_load(2 * j + i, 2 * j + i).start()
            return carry

        lax.fori_loop(0, chunks, body, 0)
        def act(j, carry):
            pair_copy(s, j).wait_recv()
            gate = own_sums[j, 0] + recv_sums[s, j, 0].astype(F32)
            up = own_sums[j, 1] + recv_sums[s, j, 1].astype(F32)
            hidden[j] = (gate / (1.0 + jnp.exp(-gate)) * up).astype(BF16)
            return carry

        lax.fori_loop(0, chunks, act, 0)

    freed = min(2 * chunks, strips - RING)

    def down(s):
        def body(e, carry):
            if s == 0:
                j = e
                slot = 2 * chunks + e % RING
                down_load(j, slot).wait()
            else:
                j = (e + strips - RING) % strips
                resident = 2 * chunks + j % RING
                slot = jnp.where(e < RING, resident, (e - RING) % freed)

                @pl.when(e >= RING)
                def _():
                    down_load(j, slot).wait()

            h = jnp.concatenate([hidden[c] for c in range(chunks)], axis=1)
            part = jnp.dot(h, pool[slot, pl.ds(0, units), pl.ds(0, STRIP)], preferred_element_type=F32)
            if s == 0:
                @pl.when(e + RING < strips)
                def _():
                    down_load(e + RING, slot).start()
            elif freed < strips - RING:
                @pl.when((e >= RING) & (e + freed < strips))
                def _():
                    down_load(e - RING + freed, slot).start()
            value = part.astype(BF16)
            for rb in range(row_blocks):
                part_send[s, j, rb] = value[rb * block_rows:(rb + 1) * block_rows]
            group = strip_block(j)

            def send(r, carry):
                rb = (my_row_block + 1 + r) % row_blocks
                owner = rb * groups + group

                @pl.when(owner != me)
                def _():
                    part_copy(s, j, rb, owner, me).start()

                @pl.when(owner == me)
                def _():
                    part_recv[s, me, j % halves] = part_send[s, j, rb]

                return carry

            lax.fori_loop(0, row_blocks, send, 0)
            return carry

        lax.fori_loop(0, strips, body, 0)

    def reduce(s, h):
        def body(i, total):
            source = (me + n - i) % n
            part_copy(s, h, 0, source, source).wait_recv()
            return total + part_recv[s, source, h].astype(F32)

        return lax.fori_loop(1, n, body, part_recv[s, me, h].astype(F32))

    place_tokens(0, rows_in)
    gate_up(0)
    place_tokens(1, rows_next)
    down(0)
    for h in range(halves):
        piece[h] = reduce(0, h).astype(BF16)

        def send_piece(i, carry, h=h):
            gather_copy(h, (me + i) % n, me).start()
            return carry

        lax.fori_loop(1, n, send_piece, 0)
        mixed_all[me, h] = piece[h]

    def take(i, carry):
        source = (me + i) % n
        at = pl.ds(pl.multiple_of(source // groups * block_rows, block_rows), block_rows)
        for h in range(halves):
            @pl.when(i > 0)
            def _():
                gather_copy(h, source, source).wait_recv()

            b = source % groups * halves + h
            rows_in[b, at, :] = (
                rows_next[b, at, :].astype(F32) + mixed_all[source, h].astype(F32)
            ).astype(BF16)
        return carry

    lax.fori_loop(0, n, take, 0)

    gate_up(1)
    pick = (
        lax.broadcasted_iota(jnp.int32, (8, block_rows), 1)
        == lax.broadcasted_iota(jnp.int32, (8, block_rows), 0) + my_group * per_dev
    ).astype(F32).astype(BF16)
    for g in range(groups):
        for h in range(halves):
            mine = jnp.dot(pick, mixed_all[my_row_block * groups + g, h], preferred_element_type=F32)
            b = g * halves + h
            out_ref[0, :, b * STRIP:(b + 1) * STRIP] = mine[:per_dev].astype(BF16)
    down(1)
    for h in range(halves):
        total = reduce(1, h)
        for t in range(groups):
            tail_send[t, h] = total[t * per_dev:(t + 1) * per_dev].astype(BF16)

            @pl.when(t != my_group)
            def _():
                tail_copy(h, t, my_group).start()

        cols = pl.ds(pl.multiple_of((my_group * halves + h) * STRIP, STRIP), STRIP)
        out_ref[1, :, cols] = tail_send[my_group, h]

    for s in range(steps):
        def pair_sent(j, carry, s=s):
            pair_copy(s, j).wait_send()
            return carry

        lax.fori_loop(0, chunks, pair_sent, 0)

        def tok_sent(i, carry, s=s):
            tok_copy(s, (me + i) % n, me).wait_send()
            return carry

        lax.fori_loop(1, n, tok_sent, 0)

        def part_sent(j, carry, s=s):
            for rb in range(row_blocks):
                owner = rb * groups + strip_block(j)

                @pl.when(owner != me)
                def _():
                    part_copy(s, j, rb, owner, me).wait_send()

            return carry

        lax.fori_loop(0, strips, part_sent, 0)

    def piece_sent(i, carry):
        for h in range(halves):
            gather_copy(h, (me + i) % n, me).wait_send()
        return carry

    lax.fori_loop(1, n, piece_sent, 0)
    for h in range(halves):
        for t in range(groups):
            @pl.when(t != my_group)
            def _():
                tail_copy(h, t, my_group).wait_send()
                tail_copy(h, t, t).wait_recv()


def on_device(n, tokens, gate_weight, up_weight, down_weight):
    steps, per_dev, width = tokens.shape
    units = gate_weight.shape[1]
    unit_tile = 256 if units % 256 == 0 else units
    chunks = units // unit_tile
    groups = min(n, 8)
    halves = width // groups // STRIP
    strips = width // STRIP
    row_blocks = n // groups
    rows = n * per_dev
    block_rows = per_dev * groups
    dma = pltpu.SemaphoreType.DMA
    slots = 2 * chunks + RING
    scratch = [
        pltpu.VMEM((slots, max(width, units), max(unit_tile, STRIP)), BF16),
        pltpu.VMEM((steps, n, per_dev, width), BF16),
        pltpu.VMEM((strips, rows, STRIP), BF16),
        pltpu.VMEM((strips, rows, STRIP), BF16),
        pltpu.VMEM((chunks, 2, rows, unit_tile), F32),
        pltpu.VMEM((steps, chunks, 2, rows, unit_tile), BF16),
        pltpu.VMEM((steps, chunks, 2, rows, unit_tile), BF16),
        pltpu.VMEM((chunks, rows, unit_tile), BF16),
        pltpu.VMEM((steps, strips, row_blocks, block_rows, STRIP), BF16),
        pltpu.VMEM((steps, n, halves, block_rows, STRIP), BF16),
        pltpu.VMEM((halves, block_rows, STRIP), BF16),
        pltpu.VMEM((n, halves, block_rows, STRIP), BF16),
        pltpu.VMEM((groups, halves, per_dev, STRIP), BF16),
        dma((slots,)),
        dma((steps,)),
        dma((steps, n)),
        dma((steps, n)),
        dma((steps, chunks)),
        dma((steps, chunks)),
        dma((steps, strips, row_blocks)),
        dma((steps, n, halves)),
        dma((n, halves)),
        dma((n, halves)),
        dma((groups, halves)),
        dma((groups, halves)),
    ]
    hbm = pl.BlockSpec(memory_space=pl.ANY)
    return pl.pallas_call(
        functools.partial(kernel, n, groups, halves, unit_tile),
        out_shape=jax.ShapeDtypeStruct(tokens.shape, BF16),
        in_specs=[hbm] * 4,
        out_specs=pl.BlockSpec(memory_space=pltpu.VMEM),
        scratch_shapes=scratch,
        compiler_params=pltpu.CompilerParams(
            collective_id=0, has_side_effects=True, vmem_limit_bytes=64 * 1024 * 1024
        ),
    )(tokens, gate_weight, up_weight, down_weight)


def solution(mesh):
    in_specs = (
        P(None, ("grp", "wide"), "narrow"),
        P("narrow", "wide"),
        P("narrow", "wide"),
        P("wide", "narrow"),
    )
    return jax.shard_map(
        functools.partial(on_device, mesh.shape["wide"]),
        mesh=mesh,
        in_specs=in_specs,
        out_specs=P(None, ("grp", "wide"), "narrow"),
        check_vma=False,
    )
```

```python
import functools

import jax
import jax.numpy as jnp
from jax import lax
from jax.experimental import pallas as pl
from jax.experimental.pallas import tpu as pltpu
from jax.sharding import PartitionSpec as P

F32 = jnp.float32
BF16 = jnp.bfloat16
MESH = pl.DeviceIdType.MESH
STRIP = 256
AHEAD = 4
LAG = (3, 8)
QUARTERS = 4
RING = 4


def kernel(
    n, unit_tile, tok_ref, gate_ref, up_ref, down_ref, out_ref,
    pool, ring, tok_all, tok_next, rows_in, own_sums, send_sums, recv_sums, hidden,
    part_send, part_recv, rows_all,
    load_sem, ring_sem, tok_own_sem, tok_send_sem, tok_recv_sem, pair_send_sem, pair_recv_sem,
    part_send_sem, part_recv_sem, gather_send_sem, gather_recv_sem,
):
    steps, per_dev, width = tok_ref.shape
    units = gate_ref.shape[1]
    chunks = units // unit_tile
    strips = width // STRIP
    per_quarter = strips // QUARTERS
    span = width // QUARTERS
    rows = n * per_dev
    me = lax.axis_index("wide")
    core = lax.axis_index("narrow")
    peer = {"narrow": 1 - core}

    def gate_load(j):
        cols = pl.ds(pl.multiple_of(j * unit_tile, unit_tile), unit_tile)
        return [
            pltpu.make_async_copy(
                w.at[:, cols], pool.at[2 * j + i, pl.ds(0, width), pl.ds(0, unit_tile)],
                load_sem.at[2 * j + i],
            )
            for i, w in enumerate((gate_ref, up_ref))
        ]

    def down_load(j, slot):
        cols = pl.ds(pl.multiple_of(j * STRIP, STRIP), STRIP)
        return pltpu.make_async_copy(
            down_ref.at[:, cols], pool.at[slot, pl.ds(0, units), pl.ds(0, STRIP)], load_sem.at[slot]
        )

    def ring_load(j):
        cols = pl.ds(pl.multiple_of(j * STRIP, STRIP), STRIP)
        return pltpu.make_async_copy(down_ref.at[:, cols], ring.at[j % RING], ring_sem.at[j % RING])

    ahead = min(AHEAD, chunks)
    early = min(3, chunks)

    def start_gate(j, carry):
        for copy in gate_load(j):
            copy.start()
        return carry

    def loaded(j, carry):
        for copy in gate_load(j):
            copy.wait()
        later = j + ahead

        @pl.when(later < chunks)
        def _():
            start_gate(later, 0)

        @pl.when((later >= chunks) & (later < chunks + RING))
        def _():
            ring_load(later - chunks).start()

        return carry

    lax.fori_loop(0, ahead, start_gate, 0)

    barrier = pltpu.get_barrier_semaphore()

    def greet(i, carry):
        pl.semaphore_signal(barrier, inc=1, device_id={"wide": (me + i) % n}, device_id_type=MESH)
        return carry

    lax.fori_loop(1, n, greet, 0)
    pl.semaphore_signal(barrier, inc=1, device_id=peer, device_id_type=MESH)
    pl.semaphore_wait(barrier, n)

    def tok_copy(to, slot):
        return pltpu.make_async_remote_copy(
            src_ref=tok_ref.at[0], dst_ref=tok_all.at[slot],
            send_sem=tok_send_sem.at[to], recv_sem=tok_recv_sem.at[slot],
            device_id={"wide": to}, device_id_type=MESH,
        )

    def others(act):
        def one(i, carry):
            act((me + i) % n)
            return carry

        lax.fori_loop(1, n, one, 0)

    own_tokens = [
        pltpu.make_async_copy(tok_ref.at[0], tok_all.at[me], tok_own_sem.at[0]),
        pltpu.make_async_copy(tok_ref.at[1], tok_next, tok_own_sem.at[1]),
    ]

    def place(read, first):
        per = 16 // per_dev

        def one(i, carry):
            value = jnp.concatenate(
                [read(i * per + t).astype(F32) for t in range(per)], axis=0
            ).astype(BF16)
            at = pl.ds(pl.multiple_of(i * 16, 16), 16)
            for b in range(value.shape[1] // STRIP):
                rows_in[first + b, at, :] = value[:, b * STRIP:(b + 1) * STRIP]
            return carry

        lax.fori_loop(0, rows // 16, one, 0)

    def pair_copy(s, j):
        return pltpu.make_async_remote_copy(
            src_ref=send_sums.at[s, j], dst_ref=recv_sums.at[s, j],
            send_sem=pair_send_sem.at[s, j], recv_sem=pair_recv_sem.at[s, j],
            device_id=peer, device_id_type=MESH,
        )

    def part_copy(s, q, owner, slot):
        return pltpu.make_async_remote_copy(
            src_ref=part_send.at[s, q, owner], dst_ref=part_recv.at[s, q, slot],
            send_sem=part_send_sem.at[s, q, owner], recv_sem=part_recv_sem.at[s, q, slot],
            device_id={"wide": owner}, device_id_type=MESH,
        )

    def gather_copy(q, to, slot):
        return pltpu.make_async_remote_copy(
            src_ref=rows_all.at[q, me], dst_ref=rows_all.at[q, slot],
            send_sem=gather_send_sem.at[q, to], recv_sem=gather_recv_sem.at[q, slot],
            device_id={"wide": to}, device_id_type=MESH,
        )

    def gate_up_part(q):
        def tile(j):
            x = jnp.concatenate([rows_in[q * per_quarter + b] for b in range(per_quarter)], axis=1)
            for i in range(2):
                value = jnp.dot(
                    x, pool[2 * j + i, pl.ds(q * span, span), pl.ds(0, unit_tile)],
                    preferred_element_type=F32,
                )
                own_sums[j, i] = value if q == 0 else own_sums[j, i] + value

        def body(p, carry):
            for k in range(4):
                tile(4 * p + k)
            return carry

        lax.fori_loop(0, chunks // 4, body, 0)
        for j in range(chunks // 4 * 4, chunks):
            tile(j)

    def gate_up(s):
        skip = 0 if s == 0 else QUARTERS - 1

        lag = min(LAG[s], chunks)

        def act(j):
            gate = own_sums[j, 0] + recv_sums[s, j, 0].astype(F32)
            up = own_sums[j, 1] + recv_sums[s, j, 1].astype(F32)
            hidden[j] = (gate / (1.0 + jnp.exp(-gate)) * up).astype(BF16)

        def body(j, carry, active):
            if s == 0:
                @pl.when(j >= early)
                def _():
                    loaded(j, 0)
            if active:
                pair_copy(s, j - lag).wait_recv()
                act(j - lag)
            x = jnp.concatenate([rows_in[b] for b in range(skip * per_quarter, strips)], axis=1)
            sums = [
                jnp.dot(
                    x, pool[2 * j + i, pl.ds(skip * span, width - skip * span), pl.ds(0, unit_tile)],
                    preferred_element_type=F32,
                )
                for i in range(2)
            ]
            if skip:
                sums = [own_sums[j, i] + sums[i] for i in range(2)]
            for i in range(2):
                own_sums[j, i] = sums[i]
                send_sums[s, j, i] = sums[i].astype(BF16)
            pair_copy(s, j).start()
            if s == 1:
                for i in range(2):
                    @pl.when(2 * j + i < strips - RING)
                    def _():
                        down_load(2 * j + i, 2 * j + i).start()
            return carry

        lax.fori_loop(0, lag, functools.partial(body, active=False), 0)
        if chunks > lag:
            lax.fori_loop(lag, chunks, functools.partial(body, active=True), 0)
        if s == 0:
            for d in range(ahead, RING):
                ring_load(d).start()
        for j in range(chunks - lag, chunks):
            pair_copy(s, j).wait_recv()
            act(j)

    freed = min(2 * chunks, strips - RING)

    def down(s):
        def two(p, first, strip_of, started):
            h = jnp.concatenate([hidden[c] for c in range(chunks)], axis=1)
            strip = [first + 2 * p + i for i in range(2)]
            parts = [jnp.dot(h, strip_of(j), preferred_element_type=F32) for j in strip]
            for j in strip:
                started(j)
            q = strip[0] // per_quarter
            for j, part in zip(strip, parts):
                at = pl.ds(pl.multiple_of(j % per_quarter * STRIP, STRIP), STRIP)
                for d in range(n):
                    part_send[s, q, d, :, at] = part[d * per_dev:(d + 1) * per_dev].astype(BF16)

            @pl.when(p % (per_quarter // 2) == per_quarter // 2 - 1)
            def _():
                others(lambda to: part_copy(s, q, to, me).start())

        def through_ring(p, carry):
            for i in range(2):
                ring_load(2 * p + i).wait()

            def more(j):
                @pl.when(j + RING < strips)
                def _():
                    ring_load(j + RING).start()

            two(p, 0, lambda j: ring[j % RING], more)
            return carry

        def from_ring(p, carry):
            two(p, strips - RING, lambda j: ring[j % RING], lambda j: None)
            return carry

        def from_pool(p, carry):
            for i in range(2):
                down_load(2 * p + i, (2 * p + i) % freed).wait()

            def more(j):
                if freed < strips - RING:
                    @pl.when(j + freed < strips - RING)
                    def _():
                        down_load(j + freed, j % freed).start()

            two(p, 0, lambda j: pool[j % freed, pl.ds(0, units), pl.ds(0, STRIP)], more)
            return carry

        if s == 0:
            lax.fori_loop(0, strips // 2, through_ring, 0)
        else:
            lax.fori_loop(0, RING // 2, from_ring, 0)
            lax.fori_loop(0, (strips - RING) // 2, from_pool, 0)

    def reduce(s, q):
        def body(i, total):
            source = (me + i) % n
            part_copy(s, q, source, source).wait_recv()
            return total + part_recv[s, q, source].astype(F32)

        mixed = lax.fori_loop(1, n, body, part_send[s, q, me].astype(F32)).astype(BF16)
        out_ref[s, :, q * span:(q + 1) * span] = mixed
        return mixed

    for copy in own_tokens:
        copy.start()
    others(lambda to: tok_copy(to, me).start())
    lax.fori_loop(0, early, loaded, 0)
    for copy in own_tokens:
        copy.wait()
    others(lambda source: tok_copy(source, source).wait_recv())
    place(lambda i: tok_all[i], 0)
    gate_up(0)
    down(0)

    def hand_on(q):
        mixed = reduce(0, q)
        new = tok_next[:, q * span:(q + 1) * span].astype(F32)
        rows_all[q, me] = (new + mixed.astype(F32)).astype(BF16)
        others(lambda to: gather_copy(q, to, me).start())

    def take(q):
        others(lambda source: gather_copy(q, source, source).wait_recv())
        place(lambda i: rows_all[q, i], q * per_quarter)

    for q in range(QUARTERS - 1):
        hand_on(q)

    for q in range(QUARTERS - 1):
        take(q)
        gate_up_part(q)
        if q == 0:
            hand_on(QUARTERS - 1)
    take(QUARTERS - 1)
    gate_up(1)
    down(1)
    for q in range(QUARTERS):
        reduce(1, (q + QUARTERS - 1) % QUARTERS)

    for s in range(steps):
        def pair_sent(j, carry, s=s):
            pair_copy(s, j).wait_send()
            return carry

        lax.fori_loop(0, chunks, pair_sent, 0)

        for q in range(QUARTERS):
            others(lambda to: part_copy(s, q, to, me).wait_send())
    others(lambda to: tok_copy(to, me).wait_send())
    for q in range(QUARTERS):
        others(lambda to: gather_copy(q, to, me).wait_send())


def on_device(n, tokens, gate_weight, up_weight, down_weight):
    steps, per_dev, width = tokens.shape
    units = gate_weight.shape[1]
    unit_tile = 256 if units % 256 == 0 else units
    chunks = units // unit_tile
    groups = min(n, 8)
    strips = width // STRIP
    rows = n * per_dev
    span = width // QUARTERS
    dma = pltpu.SemaphoreType.DMA
    slots = 2 * chunks
    scratch = [
        pltpu.VMEM((slots, max(width, units), max(unit_tile, STRIP)), BF16),
        pltpu.VMEM((RING, units, STRIP), BF16),
        pltpu.VMEM((n, per_dev, width), BF16),
        pltpu.VMEM((per_dev, width), BF16),
        pltpu.VMEM((strips, rows, STRIP), BF16),
        pltpu.VMEM((chunks, 2, rows, unit_tile), F32),
        pltpu.VMEM((steps, chunks, 2, rows, unit_tile), BF16),
        pltpu.VMEM((steps, chunks, 2, rows, unit_tile), BF16),
        pltpu.VMEM((chunks, rows, unit_tile), BF16),
        pltpu.VMEM((steps, QUARTERS, n, per_dev, span), BF16),
        pltpu.VMEM((steps, QUARTERS, n, per_dev, span), BF16),
        pltpu.VMEM((QUARTERS, n, per_dev, span), BF16),
        dma((slots,)),
        dma((RING,)),
        dma((2,)),
        dma((n,)),
        dma((n,)),
        dma((steps, chunks)),
        dma((steps, chunks)),
        dma((steps, QUARTERS, n)),
        dma((steps, QUARTERS, n)),
        dma((QUARTERS, n)),
        dma((QUARTERS, n)),
    ]
    hbm = pl.BlockSpec(memory_space=pl.ANY)
    return pl.pallas_call(
        functools.partial(kernel, n, unit_tile),
        out_shape=jax.ShapeDtypeStruct(tokens.shape, BF16),
        in_specs=[hbm] * 4,
        out_specs=pl.BlockSpec(memory_space=pltpu.VMEM),
        scratch_shapes=scratch,
        compiler_params=pltpu.CompilerParams(
            collective_id=0, has_side_effects=True, vmem_limit_bytes=64 * 1024 * 1024
        ),
    )(tokens, gate_weight, up_weight, down_weight)


def solution(mesh):
    in_specs = (
        P(None, ("grp", "wide"), "narrow"),
        P("narrow", "wide"),
        P("narrow", "wide"),
        P("wide", "narrow"),
    )
    return jax.shard_map(
        functools.partial(on_device, mesh.shape["wide"]),
        mesh=mesh,
        in_specs=in_specs,
        out_specs=P(None, ("grp", "wide"), "narrow"),
        check_vma=False,
    )
```
